32 devices in a mesh: beam: 2 (over y), chan: 4 (over z), tgrp: 2 (over x), pol: 2 (over core).
Axes of the slice: x: 2, y: 2, z: 4, core: 2. Of those that a mesh axis runs over, the one named last changes fastest.
Arguments:
- voltages: bfloat16 [16, 8192, 512], P(('beam', 'chan', 'tgrp'), None, 'pol'), parts along dimension 0, may hold values from -6 to 6
- filter_taps: float32 [4, 8192], replicated, may hold values from -0.03125 to 0.03125
Outputs:
- visibility: float32 [512, 16, 2, 512], P('tgrp', ('beam', 'chan'), None, 'pol'), parts along dimension 1
The draws below stay inside these ranges and needn't reach their ends.
There are 2 independent parts, one for each index of `beam`. The reference program is written for one: setup_inputs(seed, part) draws one part's arguments, and reference() takes and returns one part's arrays. A program takes and returns all parts, laid end to end along the dimension named above; an argument that names none is the same for every part. Nothing has to cross between parts.
All inputs are finite; a program needn't handle non-finite values.
Results may differ from the reference program's by a relative error of at most 0.013.
Values may be sent and summed in bfloat16 or wider, within the bound.
No kernel may reach another device: no remote copies, remote signals or barrier semaphores. Data moves between devices by JAX's collectives and lax.ppermute only.
A program may use at most 64 MiB of HBM per device.

```python
import jax
import jax.numpy as jnp
from jax import lax

LEN = 8192
INPUTS = 512
TAPS = 4
BAND_START = 1024
BAND = 8
FRAMES = 8


def block_scale(own_key, shape, cuts, least, largest):
    def one(position, shards_of):
        draws = jax.random.uniform(jax.random.fold_in(jax.random.fold_in(own_key, 6), position), (shards_of,), jnp.float32, least / len(cuts), largest / len(cuts))
        return jnp.repeat(jnp.exp(draws), shape[position] // shards_of).reshape((-1,) + (1,) * (len(shape) - position - 1))

    gain = one(*cuts[0])
    for cut in cuts[1:]:
        gain = gain * one(*cut)
    return gain


def centred(key, dims, width, bound, shards=(), held_as=jnp.bfloat16):
    result = width * jax.random.normal(key, dims, jnp.float32)
    if shards:
        result = result * block_scale(key, dims, shards, -0.22, 0.18)
    return jnp.clip(result, -bound, bound).astype(held_as)


def setup_inputs(seed: int = 0, part: int = 0) -> dict:
    key_of = jax.random.split(jax.random.key(seed), 3)
    part_splits = jax.random.split(jax.random.fold_in(key_of[2], part), 3)
    return {
        "voltages": centred(part_splits[0], (FRAMES, LEN, INPUTS), 1.0, 6.0, ((0, 8), (2, 2))),
        "filter_taps": centred(key_of[1], (TAPS, LEN), (TAPS * LEN) ** -0.5, 0.03125, (), jnp.float32),
    }


def reference(voltages, filter_taps):
    frames, length, inputs = voltages.shape
    lead_count = TAPS - 1

    def one_frame(frame_index):
        windowed = jnp.zeros((length, inputs), jnp.float32)
        for tap_index in range(TAPS):
            source = frame_index - lead_count + tap_index
            picked = lax.dynamic_index_in_dim(voltages, jnp.maximum(source, 0).astype(jnp.int32), 0, keepdims=False)
            weight = jnp.where(source >= 0, 1.0, 0.0).astype(jnp.float32)
            windowed = windowed + weight * filter_taps[tap_index][:, None] * picked.astype(jnp.float32)
        spectrum = jnp.fft.rfft(windowed, axis=0)[BAND_START:BAND_START + BAND]
        return jnp.stack([jnp.real(spectrum), jnp.imag(spectrum)], 0).astype(jnp.bfloat16)

    spectra = lax.map(one_frame, jnp.arange(frames, dtype=jnp.int32))
    wide_spectra = spectra.astype(jnp.float32)
    real_part = jnp.einsum("frki,frkj->ikj", wide_spectra, wide_spectra)
    imag_part = jnp.einsum("fki,fkj->ikj", wide_spectra[:, 1], wide_spectra[:, 0]) - jnp.einsum("fki,fkj->ikj", wide_spectra[:, 0], wide_spectra[:, 1])
    return jnp.stack([real_part, imag_part], 2) * (1.0 / FRAMES)
```

```python
import functools
import math

import jax
import jax.numpy as jnp
import numpy as np
from jax import lax
from jax.experimental import pallas as pl
from jax.experimental.pallas import tpu as pltpu
from jax.sharding import PartitionSpec as P

BAND_START = 1024
CH_DEV = 2
PARTS = 2
LANES = 128


def twiddle_table(length, blocks):
    channel = BAND_START + np.arange(blocks * CH_DEV, dtype=np.int64)
    phase = (channel[:, None] * np.arange(length, dtype=np.int64)) % length
    angles = phase * (2.0 * math.pi / length)
    table = np.stack([np.cos(angles), -np.sin(angles)], 0)
    table = table.reshape(PARTS, blocks, CH_DEV, length).transpose(1, 0, 2, 3)
    return table.reshape(blocks * PARTS * CH_DEV, length).astype(np.float32)


def transform_kernel(chunk, voltages_hbm, taps_ref, twiddle_hbm, out_ref, volts, table, sems):
    chunks = volts.shape[0] // chunk
    taps = taps_ref.shape[0]
    rows = table.shape[0]

    def copies(step):
        part = pl.ds(step * chunk, chunk)
        return (
            pltpu.make_async_copy(twiddle_hbm.at[:, part], table.at[:, part], sems.at[0, step]),
            pltpu.make_async_copy(voltages_hbm.at[part], volts.at[part], sems.at[1, step]),
        )

    for step in range(chunks):
        for copy in copies(step):
            copy.start()
    total = jnp.zeros((taps * rows, volts.shape[1]), jnp.float32)
    for step in range(chunks):
        part = pl.ds(step * chunk, chunk)
        table_copy, volts_copy = copies(step)
        table_copy.wait()
        turns = table[:, part]
        weights = jnp.concatenate([turns * taps_ref[t:t + 1, part] for t in range(taps)], 0)
        high = weights.astype(jnp.bfloat16)
        low = (weights - high.astype(jnp.float32)).astype(jnp.bfloat16)
        volts_copy.wait()
        both = jnp.dot(jnp.concatenate([high, low], 0), volts[part], preferred_element_type=jnp.float32)
        total = total + (both[:taps * rows] + both[taps * rows:])
    per_block = PARTS * CH_DEV
    blocks = rows // per_block
    pieces = [
        total[t * rows + b * per_block:t * rows + (b + 1) * per_block]
        for b in range(blocks)
        for t in range(taps)
    ]
    out_ref[...] = jnp.concatenate(pieces, 0).astype(out_ref.dtype)


def transform(voltages, filter_taps, twiddle):
    length, inputs = voltages.shape
    taps = filter_taps.shape[0]
    rows = twiddle.shape[0]
    chunk = min(length, 1024)
    chunks = length // chunk
    return pl.pallas_call(
        functools.partial(transform_kernel, chunk),
        out_shape=jax.ShapeDtypeStruct((taps * rows, inputs), jnp.bfloat16),
        in_specs=[
            pl.BlockSpec(memory_space=pltpu.HBM),
            pl.BlockSpec(memory_space=pltpu.VMEM),
            pl.BlockSpec(memory_space=pltpu.HBM),
        ],
        out_specs=pl.BlockSpec(memory_space=pltpu.VMEM),
        scratch_shapes=[
            pltpu.VMEM((length, inputs), jnp.bfloat16),
            pltpu.VMEM((rows, length), jnp.float32),
            pltpu.SemaphoreType.DMA((2, chunks)),
        ],
        compiler_params=pltpu.CompilerParams(vmem_limit_bytes=62 * 2**20),
        name="transform",
    )(voltages, filter_taps, twiddle)


def spectra_of(terms, taps):
    frames = terms.shape[0]
    per_tap = PARTS * CH_DEV
    spectra = []
    for frame in range(frames):
        total = None
        for tap in range(taps):
            source = frame - (taps - 1) + tap
            if source >= 0:
                term = terms[source, tap * per_tap:(tap + 1) * per_tap].astype(jnp.float32)
                total = term if total is None else total + term
        spectra.append(total.astype(jnp.bfloat16))
    return spectra


def power_kernel(taps, scale, left_ref, right_ref, out_ref):
    left = spectra_of(left_ref[...], taps)
    right = spectra_of(right_ref[...], taps)
    rows = left_ref.shape[2]
    step = 2 * CH_DEV * PARTS
    for channel in range(CH_DEV):
        a = [s[r * CH_DEV + channel:r * CH_DEV + channel + 1] for r in range(PARTS) for s in left]
        b = [s[r * CH_DEV + channel:r * CH_DEV + channel + 1] for r in range(PARTS) for s in right]
        half = len(b) // 2
        turned = [-x for x in b[half:]] + b[:half]
        a = jnp.concatenate(a, 0)
        for part, other in ((0, b), (1, turned)):
            product = scale * lax.dot_general(
                a, jnp.concatenate(other, 0), (((0,), (0,)), ((), ())), preferred_element_type=jnp.float32
            )
            for tile in range(product.shape[1] // LANES):
                start = (channel * (product.shape[1] // LANES) + tile) * PARTS + part
                out_ref[pl.ds(start, rows, stride=out_ref.shape[0] // rows), :] = product[
                    :, tile * LANES:(tile + 1) * LANES
                ]


def powers(left, right, taps, frames):
    rows, columns = left.shape[2], right.shape[2]
    tiles = columns // LANES
    out = pl.pallas_call(
        functools.partial(power_kernel, taps, 1.0 / frames),
        out_shape=jax.ShapeDtypeStruct((rows * CH_DEV * tiles * PARTS, LANES), jnp.float32),
        in_specs=[pl.BlockSpec(memory_space=pltpu.VMEM)] * 2,
        out_specs=pl.BlockSpec(memory_space=pltpu.VMEM),
        compiler_params=pltpu.CompilerParams(vmem_limit_bytes=32 * 2**20),
        name="powers",
    )(left, right)
    out = out.reshape(rows, CH_DEV, tiles, PARTS, LANES).transpose(0, 1, 3, 2, 4)
    return out.reshape(rows, CH_DEV, PARTS, columns)


def body(voltages, filter_taps):
    taps = filter_taps.shape[0]
    chans, groups = lax.axis_size("chan"), lax.axis_size("tgrp")
    frames = chans * groups
    twiddle = jnp.asarray(twiddle_table(voltages.shape[1], chans))
    terms = transform(voltages[0], filter_taps, twiddle)
    terms = terms.reshape(chans, 1, -1, terms.shape[1])
    terms = jnp.broadcast_to(terms, (chans, groups) + terms.shape[2:]).reshape((frames,) + terms.shape[2:])
    turned = lax.all_to_all(terms, ("chan", "tgrp"), split_axis=0, concat_axis=0, tiled=True)
    gathered = lax.all_gather(turned, "pol", axis=2, tiled=True)
    rows = gathered.shape[2] // groups
    left = lax.dynamic_slice_in_dim(gathered, lax.axis_index("tgrp") * rows, rows, 2)
    return powers(left, turned, taps, frames)


def solution(mesh):
    return jax.shard_map(
        body,
        mesh=mesh,
        in_specs=(P(("beam", "chan", "tgrp"), None, "pol"), P()),
        out_specs=P("tgrp", ("beam", "chan"), None, "pol"),
        check_vma=False,
    )
```

```python
import functools
import math

import jax
import jax.numpy as jnp
import numpy as np
from jax import lax
from jax.experimental import pallas as pl
from jax.experimental.pallas import tpu as pltpu
from jax.sharding import PartitionSpec as P

BAND_START = 1024
CH_DEV = 2
PARTS = 2
LANES = 128
AXES = ("chan", "tgrp", "pol")


def twiddle_table(length, blocks):
    channel = BAND_START + np.arange(blocks * CH_DEV, dtype=np.int64)
    phase = (channel[:, None] * np.arange(length, dtype=np.int64)) % length
    angles = phase * (2.0 * math.pi / length)
    table = np.stack([np.cos(angles), -np.sin(angles)], 0)
    table = table.reshape(PARTS, blocks, CH_DEV, length).transpose(1, 0, 2, 3)
    return table.reshape(blocks * PARTS * CH_DEV, length).astype(np.float32)


def transform_kernel(chunk, voltages_hbm, taps_hbm, twiddle_hbm, out_ref, volts, taps_ref, table, weights, sems):
    length = volts.shape[0]
    chunks = length // chunk
    taps = taps_ref.shape[0]
    rows = table.shape[0]
    per_block = PARTS * CH_DEV
    blocks = rows // per_block
    taps_copy = pltpu.make_async_copy(taps_hbm, taps_ref, sems.at[0])
    table_copy = pltpu.make_async_copy(twiddle_hbm, table, sems.at[1])
    taps_copy.start()
    table_copy.start()
    volts_copies = [
        pltpu.make_async_copy(
            voltages_hbm.at[pl.ds(step * chunk, chunk)], volts.at[pl.ds(step * chunk, chunk)], sems.at[2 + step]
        )
        for step in range(chunks)
    ]
    for copy in volts_copies:
        copy.start()
    taps_copy.wait()
    table_copy.wait()
    for step in range(chunks):
        part = pl.ds(step * chunk, chunk)
        turns = table[:, part]
        for t in range(taps):
            exact = turns * taps_ref[t:t + 1, part]
            high = exact.astype(jnp.bfloat16)
            weights[t * rows:(t + 1) * rows, part] = high
            weights[(taps + t) * rows:(taps + t + 1) * rows, part] = (
                exact - high.astype(jnp.float32)
            ).astype(jnp.bfloat16)
    total = jnp.zeros((2 * taps * rows, volts.shape[1]), jnp.float32)
    for step in range(chunks):
        part = pl.ds(step * chunk, chunk)
        volts_copies[step].wait()
        total = total + jnp.dot(weights[:, part], volts[part], preferred_element_type=jnp.float32)
    total = total[:taps * rows] + total[taps * rows:]
    mine = lax.axis_index("chan")
    for block in range(blocks):
        pieces = [
            total[t * rows + block * per_block:t * rows + (block + 1) * per_block] for t in range(taps)
        ]
        out_ref[lax.bitwise_xor(mine, block)] = jnp.concatenate(pieces, 0).astype(out_ref.dtype)


def transform(voltages, filter_taps, twiddle):
    length, inputs = voltages.shape
    taps = filter_taps.shape[0]
    rows = twiddle.shape[0]
    chunk = min(length, 1024)
    chunks = length // chunk
    per_block = PARTS * CH_DEV
    return pl.pallas_call(
        functools.partial(transform_kernel, chunk),
        out_shape=jax.ShapeDtypeStruct((rows // per_block, taps * per_block, inputs), jnp.bfloat16),
        in_specs=[pl.BlockSpec(memory_space=pltpu.HBM)] * 3,
        out_specs=pl.BlockSpec(memory_space=pltpu.VMEM),
        scratch_shapes=[
            pltpu.VMEM((length, inputs), jnp.bfloat16),
            pltpu.VMEM((taps, length), jnp.float32),
            pltpu.VMEM((rows, length), jnp.float32),
            pltpu.VMEM((2 * taps * rows, length), jnp.bfloat16),
            pltpu.SemaphoreType.DMA((2 + chunks,)),
        ],
        compiler_params=pltpu.CompilerParams(vmem_limit_bytes=int(53.8 * 2**20)),
        name="transform",
    )(voltages, filter_taps, twiddle)


def moved(array, frame_bits, swap):
    chans, groups = lax.axis_size("chan"), lax.axis_size("tgrp")
    count = chans * groups * 2
    return lax.ppermute(array, AXES, [(i, i ^ (frame_bits * 2 + swap)) for i in range(count)])


def exchanged(terms):
    chans, groups = lax.axis_size("chan"), lax.axis_size("tgrp")
    held = {(0, 0): terms}
    bits = [groups << b for b in reversed(range(chans.bit_length() - 1))]
    bits += [1 << b for b in reversed(range(groups.bit_length() - 1))]
    for bit in bits:
        if bit >= groups:
            keep = bit // groups
            sent = {key: value[keep:] for key, value in held.items()}
            held = {key: value[:keep] for key, value in held.items()}
        else:
            sent = dict(held)
        keys = list(sent)
        single = [key for key in keys if (key[0], 1 - key[1]) not in sent]
        got = moved(jnp.concatenate([sent[key] for key in keys], 0), bit, 1)
        other = moved(jnp.concatenate([held[key] for key in single], 0), 0, 1)
        depth = held[keys[0]].shape[0]
        for index, (frame, half) in enumerate(keys):
            held[frame ^ bit, 1 - half] = got[index * depth:(index + 1) * depth]
        for index, (frame, half) in enumerate(single):
            held[frame, 1 - half] = other[index * depth:(index + 1) * depth]
    single = [key for key in held if (key[0], 1 - key[1]) not in held]
    other = moved(jnp.concatenate([held[key] for key in single], 0), 0, 1)
    for index, (frame, half) in enumerate(single):
        held[frame, 1 - half] = other[index:index + 1]
    return held


def power_kernel(taps, groups, scale, order, *refs):
    piece_refs, out_ref, terms = refs[:-2], refs[-2], refs[-1]
    frames, columns = terms.shape[1], terms.shape[3]
    per_tap = PARTS * CH_DEV
    tiles = columns // LANES
    for (frame, half), ref in zip(order, piece_refs):
        terms[half, frame] = ref[0]
    group = lax.axis_index("tgrp")
    mine = lax.axis_index("chan") * groups + group
    rows = 2 * columns // groups
    left_start = group * rows
    left_half = lax.bitwise_xor(left_start // columns, lax.axis_index("pol"))

    def spectra_of(half):
        loaded = [terms[half, lax.bitwise_xor(mine, frame)].astype(jnp.float32) for frame in range(frames)]
        spectra = []
        for frame in range(frames):
            total = None
            for tap in range(taps):
                source = frame - (taps - 1) + tap
                if source >= 0:
                    term = loaded[source][tap * per_tap:(tap + 1) * per_tap]
                    total = term if total is None else total + term
            spectra.append(total)
        return spectra

    left = jnp.concatenate(spectra_of(left_half), 0)
    if rows != columns:
        left = pltpu.roll(left, columns - left_start % columns, 1)[:, :rows]
    right = spectra_of(0)
    turned = jnp.concatenate([x for s in right for x in (-s[CH_DEV:], s[:CH_DEV])], 0)
    right = jnp.concatenate(right, 0)
    channel_of = lax.broadcasted_iota(jnp.int32, right.shape, 0) % CH_DEV
    against = jnp.concatenate(
        [
            jnp.where(channel_of == channel, x, 0.0)[:, tile * LANES:(tile + 1) * LANES]
            for channel in range(CH_DEV)
            for tile in range(tiles)
            for x in (right, turned)
        ],
        1,
    ).astype(jnp.bfloat16)
    product = scale * lax.dot_general(
        left.astype(jnp.bfloat16), against, (((0,), (0,)), ((), ())), preferred_element_type=jnp.float32
    )
    per_row = CH_DEV * tiles * PARTS
    for index in range(per_row):
        out_ref[pl.ds(index, rows, stride=per_row), :] = product[:, index * LANES:(index + 1) * LANES]


def powers(held, taps):
    groups = lax.axis_size("tgrp")
    order = sorted(held)
    frames = len(order) // 2
    _, depth, columns = held[order[0]].shape
    rows = 2 * columns // groups
    tiles = columns // LANES
    out = pl.pallas_call(
        functools.partial(power_kernel, taps, groups, 1.0 / frames, order),
        out_shape=jax.ShapeDtypeStruct((rows * CH_DEV * tiles * PARTS, LANES), jnp.float32),
        in_specs=[pl.BlockSpec(memory_space=pltpu.VMEM)] * len(order),
        out_specs=pl.BlockSpec(memory_space=pltpu.VMEM),
        scratch_shapes=[pltpu.VMEM((2, frames, depth, columns), jnp.bfloat16)],
        compiler_params=pltpu.CompilerParams(vmem_limit_bytes=32 * 2**20),
        name="powers",
    )(*[held[key] for key in order])
    out = out.reshape(rows, CH_DEV, tiles, PARTS, LANES).transpose(0, 1, 3, 2, 4)
    return out.reshape(rows, CH_DEV, PARTS, columns)


def body(voltages, filter_taps):
    twiddle = jnp.asarray(twiddle_table(voltages.shape[1], lax.axis_size("chan")))
    terms = transform(voltages[0], filter_taps, twiddle)
    return powers(exchanged(terms), filter_taps.shape[0])


def solution(mesh):
    return jax.shard_map(
        body,
        mesh=mesh,
        in_specs=(P(("beam", "chan", "tgrp"), None, "pol"), P()),
        out_specs=P("tgrp", ("beam", "chan"), None, "pol"),
        check_vma=False,
    )
```

```python
import functools
import math

import jax
import jax.numpy as jnp
import numpy as np
from jax import lax
from jax.experimental import pallas as pl
from jax.experimental.pallas import tpu as pltpu
from jax.sharding import PartitionSpec as P

BAND_START = 1024
CH_DEV = 2
PARTS = 2
LANES = 128
AXES = ("chan", "tgrp", "pol")


def twiddle_table(length, blocks):
    channel = BAND_START + np.arange(blocks * CH_DEV, dtype=np.int64)
    phase = (channel[:, None] * np.arange(length, dtype=np.int64)) % length
    angles = phase * (2.0 * math.pi / length)
    table = np.stack([np.cos(angles), -np.sin(angles)], 0)
    table = table.reshape(PARTS, blocks, CH_DEV, length).transpose(1, 0, 2, 3)
    return table.reshape(blocks * PARTS * CH_DEV, length).astype(np.float32)


def transform_kernel(chunk, voltages_hbm, taps_hbm, twiddle_hbm, out_ref, volts, taps_ref, table, weights, sems):
    length = volts.shape[0]
    chunks = length // chunk
    taps = taps_ref.shape[0]
    rows = table.shape[0]
    per_block = PARTS * CH_DEV
    blocks = rows // per_block
    taps_copy = pltpu.make_async_copy(taps_hbm, taps_ref, sems.at[0])
    table_copy = pltpu.make_async_copy(twiddle_hbm, table, sems.at[1])
    taps_copy.start()
    table_copy.start()
    volts_copies = [
        pltpu.make_async_copy(
            voltages_hbm.at[pl.ds(step * chunk, chunk)], volts.at[pl.ds(step * chunk, chunk)], sems.at[2 + step]
        )
        for step in range(chunks)
    ]
    for copy in volts_copies:
        copy.start()
    taps_copy.wait()
    table_copy.wait()
    for step in range(chunks):
        part = pl.ds(step * chunk, chunk)
        turns = table[:, part]
        for t in range(taps):
            exact = turns * taps_ref[t:t + 1, part]
            high = exact.astype(jnp.bfloat16)
            weights[t * rows:(t + 1) * rows, part] = high
            weights[(taps + t) * rows:(taps + t + 1) * rows, part] = (
                exact - high.astype(jnp.float32)
            ).astype(jnp.bfloat16)
    total = jnp.zeros((2 * taps * rows, volts.shape[1]), jnp.float32)
    for step in range(chunks):
        part = pl.ds(step * chunk, chunk)
        volts_copies[step].wait()
        total = total + jnp.dot(weights[:, part], volts[part], preferred_element_type=jnp.float32)
    total = total[:taps * rows] + total[taps * rows:]
    mine = lax.axis_index("chan")
    for block in range(blocks):
        pieces = [
            total[t * rows + block * per_block:t * rows + (block + 1) * per_block] for t in range(taps)
        ]
        out_ref[lax.bitwise_xor(mine, block)] = jnp.concatenate(pieces, 0).astype(out_ref.dtype)


def transform(voltages, filter_taps, twiddle):
    length, inputs = voltages.shape
    taps = filter_taps.shape[0]
    rows = twiddle.shape[0]
    chunk = min(length, 1024)
    chunks = length // chunk
    per_block = PARTS * CH_DEV
    return pl.pallas_call(
        functools.partial(transform_kernel, chunk),
        out_shape=jax.ShapeDtypeStruct((rows // per_block, taps * per_block, inputs), jnp.bfloat16),
        in_specs=[pl.BlockSpec(memory_space=pltpu.HBM)] * 3,
        out_specs=pl.BlockSpec(memory_space=pltpu.VMEM),
        scratch_shapes=[
            pltpu.VMEM((length, inputs), jnp.bfloat16),
            pltpu.VMEM((taps, length), jnp.float32),
            pltpu.VMEM((rows, length), jnp.float32),
            pltpu.VMEM((2 * taps * rows, length), jnp.bfloat16),
            pltpu.SemaphoreType.DMA((2 + chunks,)),
        ],
        compiler_params=pltpu.CompilerParams(vmem_limit_bytes=int(53.8 * 2**20)),
        name="transform",
    )(voltages, filter_taps, twiddle)


def moved(array, frame_bits, swap):
    chans, groups = lax.axis_size("chan"), lax.axis_size("tgrp")
    count = chans * groups * 2
    return lax.ppermute(array, AXES, [(i, i ^ (frame_bits * 2 + swap)) for i in range(count)])


def exchanged(terms):
    chans, groups = lax.axis_size("chan"), lax.axis_size("tgrp")
    held = {0: (terms, 0)}
    bits = [groups << b for b in reversed(range(chans.bit_length() - 1))]
    bits += [1 << b for b in reversed(range(groups.bit_length() - 1))]
    rounds = [bits[:len(bits) % 2]] + [bits[i:i + 2] for i in range(len(bits) % 2, len(bits), 2)]
    for bits in rounds:
        of_chan = [bit for bit in bits if bit >= groups]

        def blocks_for(value, mask):
            count = value.shape[0] >> len(of_chan)
            index = sum(1 << i for i, bit in enumerate(reversed(of_chan)) if mask & bit)
            return value[index * count:(index + 1) * count]

        kept = {frame: (blocks_for(value, 0), half) for frame, (value, half) in held.items()}
        masks = [sum(bit for i, bit in enumerate(bits) if pick >> i & 1) for pick in range(1, 1 << len(bits))]
        for mask in reversed(masks):
            got = moved(jnp.concatenate([blocks_for(value, mask) for value, _ in held.values()], 0), mask, 1)
            count = got.shape[0] // len(held)
            for index, (frame, (_, half)) in enumerate(held.items()):
                kept[frame ^ mask] = (got[index * count:(index + 1) * count], 1 - half)
        held = kept
    order = sorted(held)
    return jnp.concatenate([held[frame][0] for frame in order], 0), [held[frame][1] for frame in order]


def power_kernel(taps, groups, scale, halves, had_ref, got_ref, out_ref, terms):
    frames, columns = terms.shape[1], terms.shape[3]
    per_tap = PARTS * CH_DEV
    tiles = columns // LANES
    for frame, half in enumerate(halves):
        terms[half, frame] = had_ref[frame]
        terms[1 - half, frame] = got_ref[frame]
    group = lax.axis_index("tgrp")
    mine = lax.axis_index("chan") * groups + group
    rows = 2 * columns // groups
    left_start = group * rows
    left_half = lax.bitwise_xor(left_start // columns, lax.axis_index("pol"))

    def spectra_of(half):
        loaded = [terms[half, lax.bitwise_xor(mine, frame)].astype(jnp.float32) for frame in range(frames)]
        spectra = []
        for frame in range(frames):
            total = None
            for tap in range(taps):
                source = frame - (taps - 1) + tap
                if source >= 0:
                    term = loaded[source][tap * per_tap:(tap + 1) * per_tap]
                    total = term if total is None else total + term
            spectra.append(total)
        return spectra

    left = jnp.concatenate(spectra_of(left_half), 0)
    if rows != columns:
        left = pltpu.roll(left, columns - left_start % columns, 1)[:, :rows]
    right = spectra_of(0)
    turned = jnp.concatenate([x for s in right for x in (-s[CH_DEV:], s[:CH_DEV])], 0)
    right = jnp.concatenate(right, 0)
    channel_of = lax.broadcasted_iota(jnp.int32, right.shape, 0) % CH_DEV
    against = jnp.concatenate(
        [
            jnp.where(channel_of == channel, x, 0.0)[:, tile * LANES:(tile + 1) * LANES]
            for channel in range(CH_DEV)
            for tile in range(tiles)
            for x in (right, turned)
        ],
        1,
    ).astype(jnp.bfloat16)
    product = scale * lax.dot_general(
        left.astype(jnp.bfloat16), against, (((0,), (0,)), ((), ())), preferred_element_type=jnp.float32
    )
    per_row = CH_DEV * tiles * PARTS
    for index in range(per_row):
        out_ref[pl.ds(index, rows, stride=per_row), :] = product[:, index * LANES:(index + 1) * LANES]


def powers(had, halves, taps):
    groups = lax.axis_size("tgrp")
    frames, depth, columns = had.shape
    rows = 2 * columns // groups
    tiles = columns // LANES
    out = pl.pallas_call(
        functools.partial(power_kernel, taps, groups, 1.0 / frames, halves),
        out_shape=jax.ShapeDtypeStruct((rows * CH_DEV * tiles * PARTS, LANES), jnp.float32),
        in_specs=[pl.BlockSpec(memory_space=pltpu.VMEM)] * 2,
        out_specs=pl.BlockSpec(memory_space=pltpu.VMEM),
        scratch_shapes=[pltpu.VMEM((2, frames, depth, columns), jnp.bfloat16)],
        compiler_params=pltpu.CompilerParams(vmem_limit_bytes=32 * 2**20),
        name="powers",
    )(had, moved(had, 0, 1))
    out = out.reshape(rows, CH_DEV, tiles, PARTS, LANES).transpose(0, 1, 3, 2, 4)
    return out.reshape(rows, CH_DEV, PARTS, columns)


def body(voltages, filter_taps):
    twiddle = jnp.asarray(twiddle_table(voltages.shape[1], lax.axis_size("chan")))
    terms = transform(voltages[0], filter_taps, twiddle)
    had, halves = exchanged(terms)
    return powers(had, halves, filter_taps.shape[0])


def solution(mesh):
    return jax.shard_map(
        body,
        mesh=mesh,
        in_specs=(P(("beam", "chan", "tgrp"), None, "pol"), P()),
        out_specs=P("tgrp", ("beam", "chan"), None, "pol"),
        check_vma=False,
    )
```

```python
import functools
import math

import jax
import jax.numpy as jnp
import numpy as np
from jax import lax
from jax.experimental import pallas as pl
from jax.experimental.pallas import tpu as pltpu
from jax.sharding import PartitionSpec as P

BAND_START = 1024
CH_DEV = 2
PARTS = 2
LANES = 128
CHUNK = 1024
WRITES = 4
AXES = ("chan", "tgrp", "pol")


def turn_of(samples, channels, length):
    phase = (channels[:, None] * samples) % length
    angles = phase * (2.0 * math.pi / length)
    both = np.stack([np.cos(angles), -np.sin(angles)], 0)
    return both.reshape(PARTS, -1, CH_DEV, samples.size).transpose(1, 0, 2, 3)


def twiddle_tables(length, blocks, chunk):
    channels = BAND_START + np.arange(blocks * CH_DEV, dtype=np.int64)
    first = turn_of(np.arange(chunk, dtype=np.int64), channels, length)
    crossed = np.stack([-first[:, 1], first[:, 0]], 1)
    starts = turn_of(np.arange(0, length, chunk, dtype=np.int64), channels, length)
    steps = np.concatenate([np.stack([starts[:, part]] * PARTS, 1) for part in range(PARTS)], -1)
    steps = steps.reshape(-1, steps.shape[-1])
    steps = np.pad(steps, ((0, 0), (0, -steps.shape[1] % LANES)))
    return np.concatenate([x.reshape(steps.shape[0], -1) for x in (first, crossed, steps)], 1).astype(np.float32)


def transform_kernel(chunk, voltages_hbm, taps_hbm, twiddle_hbm, out_ref, volts, taps_ref, table, weights, sems):
    length = volts.shape[0]
    chunks = length // chunk
    taps = taps_ref.shape[0]
    rows = table.shape[0]
    per_block = PARTS * CH_DEV
    blocks = rows // per_block
    table_copy = pltpu.make_async_copy(twiddle_hbm, table, sems.at[0])
    taps_copy = pltpu.make_async_copy(taps_hbm, taps_ref, sems.at[1])
    table_copy.start()
    taps_copy.start()
    volts_copies = [
        pltpu.make_async_copy(
            voltages_hbm.at[pl.ds(step * chunk, chunk)], volts.at[pl.ds(step * chunk, chunk)], sems.at[2 + step]
        )
        for step in range(chunks)
    ]
    for copy in volts_copies:
        copy.start()
    table_copy.wait()
    taps_copy.wait()
    first, crossed = table[:, :chunk], table[:, chunk:2 * chunk]
    for step in range(chunks):
        part = pl.ds(step * chunk, chunk)
        turns = first
        if step:
            turns = first * table[:, 2 * chunk + step:2 * chunk + step + 1]
            step_sin = 2 * chunk + chunks + step
            turns = turns + crossed * table[:, step_sin:step_sin + 1]
        for t in range(taps):
            exact = turns * taps_ref[t:t + 1, part]
            high = exact.astype(jnp.bfloat16)
            weights[t * rows:(t + 1) * rows, part] = high
            weights[(taps + t) * rows:(taps + t + 1) * rows, part] = (
                exact - high.astype(jnp.float32)
            ).astype(jnp.bfloat16)
    total = jnp.zeros((2 * taps * rows, volts.shape[1]), jnp.float32)
    for step in range(chunks):
        part = pl.ds(step * chunk, chunk)
        volts_copies[step].wait()
        total = total + jnp.dot(weights[:, part], volts[part], preferred_element_type=jnp.float32)
    total = total[:taps * rows] + total[taps * rows:]
    mine = lax.axis_index("chan")
    for block in range(blocks):
        pieces = [
            total[t * rows + block * per_block:t * rows + (block + 1) * per_block] for t in range(taps)
        ]
        out_ref[lax.bitwise_xor(mine, block)] = jnp.concatenate(pieces, 0).astype(out_ref.dtype)


def transform(voltages, filter_taps):
    length, inputs = voltages.shape
    taps = filter_taps.shape[0]
    chunk = min(length, CHUNK)
    chunks = length // chunk
    blocks = lax.axis_size("chan")
    twiddle = jnp.asarray(twiddle_tables(length, blocks, chunk))
    per_block = PARTS * CH_DEV
    rows = blocks * per_block
    return pl.pallas_call(
        functools.partial(transform_kernel, chunk),
        out_shape=jax.ShapeDtypeStruct((blocks, taps * per_block, inputs), jnp.bfloat16),
        in_specs=[pl.BlockSpec(memory_space=pltpu.HBM)] * 3,
        out_specs=pl.BlockSpec(memory_space=pltpu.VMEM),
        scratch_shapes=[
            pltpu.VMEM((length, inputs), jnp.bfloat16),
            pltpu.VMEM((taps, length), jnp.float32),
            pltpu.VMEM(twiddle.shape, jnp.float32),
            pltpu.VMEM((2 * taps * rows, length), jnp.bfloat16),
            pltpu.SemaphoreType.DMA((2 + chunks,)),
        ],
        compiler_params=pltpu.CompilerParams(vmem_limit_bytes=int(53.8 * 2**20)),
        name="transform",
    )(voltages, filter_taps, twiddle)


def moved(array, frame_bits, swap):
    chans, groups = lax.axis_size("chan"), lax.axis_size("tgrp")
    count = chans * groups * 2
    return lax.ppermute(array, AXES, [(i, i ^ (frame_bits * 2 + swap)) for i in range(count)])


def exchanged(terms):
    chans, groups = lax.axis_size("chan"), lax.axis_size("tgrp")
    held = {0: (terms, 0)}
    bits = [groups << b for b in reversed(range(chans.bit_length() - 1))]
    bits += [1 << b for b in reversed(range(groups.bit_length() - 1))]
    rounds = [bits[:len(bits) % 2]] + [bits[i:i + 2] for i in range(len(bits) % 2, len(bits), 2)]
    for bits in rounds:
        of_chan = [bit for bit in bits if bit >= groups]

        def blocks_for(value, mask):
            count = value.shape[0] >> len(of_chan)
            index = sum(1 << i for i, bit in enumerate(reversed(of_chan)) if mask & bit)
            return value[index * count:(index + 1) * count]

        kept = {frame: (blocks_for(value, 0), half) for frame, (value, half) in held.items()}
        masks = [sum(bit for i, bit in enumerate(bits) if pick >> i & 1) for pick in range(1, 1 << len(bits))]
        for mask in reversed(masks):
            got = moved(jnp.concatenate([blocks_for(value, mask) for value, _ in held.values()], 0), mask, 1)
            count = got.shape[0] // len(held)
            for index, (frame, (_, half)) in enumerate(held.items()):
                kept[frame ^ mask] = (got[index * count:(index + 1) * count], 1 - half)
        held = kept
    order = sorted(held)
    return jnp.concatenate([held[frame][0] for frame in order], 0), [held[frame][1] for frame in order]


def power_kernel(taps, groups, scale, halves, had_ref, got_ref, out_hbm, terms, made, sems):
    frames, columns = terms.shape[1], terms.shape[3]
    per_tap = PARTS * CH_DEV
    tiles = columns // LANES
    for frame, half in enumerate(halves):
        terms[half, frame] = had_ref[frame]
        terms[1 - half, frame] = got_ref[frame]
    group = lax.axis_index("tgrp")
    mine = lax.axis_index("chan") * groups + group
    rows = 2 * columns // groups
    left_start = group * rows
    left_half = lax.bitwise_xor(left_start // columns, lax.axis_index("pol"))

    def spectra_of(half):
        loaded = [terms[half, lax.bitwise_xor(mine, frame)].astype(jnp.float32) for frame in range(frames)]
        spectra = []
        for frame in range(frames):
            total = None
            for tap in range(taps):
                source = frame - (taps - 1) + tap
                if source >= 0:
                    term = loaded[source][tap * per_tap:(tap + 1) * per_tap]
                    total = term if total is None else total + term
            spectra.append(total)
        return spectra

    left = jnp.concatenate(spectra_of(left_half), 0)
    if rows != columns:
        left = pltpu.roll(left, columns - left_start % columns, 1)[:, :rows]
    right = spectra_of(0)
    turned = jnp.concatenate([x for s in right for x in (-s[CH_DEV:], s[:CH_DEV])], 0)
    right = jnp.concatenate(right, 0)
    channel_of = lax.broadcasted_iota(jnp.int32, right.shape, 0) % CH_DEV
    against = jnp.concatenate(
        [
            jnp.where(channel_of == channel, x, 0.0)[:, tile * LANES:(tile + 1) * LANES]
            for channel in range(CH_DEV)
            for tile in range(tiles)
            for x in (right, turned)
        ],
        1,
    ).astype(jnp.bfloat16)
    left = left.astype(jnp.bfloat16)
    per_row = CH_DEV * tiles * PARTS
    part_rows = max(rows // WRITES, 8)
    copies = []
    for step in range(rows // part_rows):
        product = scale * lax.dot_general(
            left[:, step * part_rows:(step + 1) * part_rows],
            against,
            (((0,), (0,)), ((), ())),
            preferred_element_type=jnp.float32,
        )
        start = step * part_rows * per_row
        for index in range(per_row):
            made[pl.ds(start + index, part_rows, stride=per_row), :] = product[:, index * LANES:(index + 1) * LANES]
        span = pl.ds(start, part_rows * per_row)
        copies.append(pltpu.make_async_copy(made.at[span], out_hbm.at[span], sems.at[step]))
        copies[-1].start()
    for copy in copies:
        copy.wait()


def powers(had, halves, taps):
    groups = lax.axis_size("tgrp")
    frames, depth, columns = had.shape
    rows = 2 * columns // groups
    tiles = columns // LANES
    out = pl.pallas_call(
        functools.partial(power_kernel, taps, groups, 1.0 / frames, halves),
        out_shape=jax.ShapeDtypeStruct((rows * CH_DEV * tiles * PARTS, LANES), jnp.float32),
        in_specs=[pl.BlockSpec(memory_space=pltpu.VMEM)] * 2,
        out_specs=pl.BlockSpec(memory_space=pltpu.HBM),
        scratch_shapes=[
            pltpu.VMEM((2, frames, depth, columns), jnp.bfloat16),
            pltpu.VMEM((rows * CH_DEV * tiles * PARTS, LANES), jnp.float32),
            pltpu.SemaphoreType.DMA((WRITES,)),
        ],
        compiler_params=pltpu.CompilerParams(vmem_limit_bytes=32 * 2**20),
        name="powers",
    )(had, moved(had, 0, 1))
    out = out.reshape(rows, CH_DEV, tiles, PARTS, LANES).transpose(0, 1, 3, 2, 4)
    return out.reshape(rows, CH_DEV, PARTS, columns)


def body(voltages, filter_taps):
    terms = transform(voltages[0], filter_taps)
    had, halves = exchanged(terms)
    return powers(had, halves, filter_taps.shape[0])


def solution(mesh):
    return jax.shard_map(
        body,
        mesh=mesh,
        in_specs=(P(("beam", "chan", "tgrp"), None, "pol"), P()),
        out_specs=P("tgrp", ("beam", "chan"), None, "pol"),
        check_vma=False,
    )
```

```python
import functools
import math

import jax
import jax.numpy as jnp
import numpy as np
from jax import lax
from jax.experimental import pallas as pl
from jax.experimental.pallas import tpu as pltpu
from jax.sharding import PartitionSpec as P

BAND_START = 1024
CH_DEV = 2
PARTS = 2
LANES = 128
CHUNK = 1024
ENDS = (1, 3, 6, 8)
WRITES = 4
AXES = ("chan", "tgrp", "pol")


def turn_of(samples, channels, length):
    phase = (channels[:, None] * samples) % length
    angles = phase * (2.0 * math.pi / length)
    both = np.stack([np.cos(angles), -np.sin(angles)], 0)
    return both.reshape(PARTS, -1, CH_DEV, samples.size).transpose(1, 0, 2, 3)


def twiddle_tables(length, blocks, chunk):
    channels = BAND_START + np.arange(blocks * CH_DEV, dtype=np.int64)
    first = turn_of(np.arange(chunk, dtype=np.int64), channels, length)
    crossed = np.stack([-first[:, 1], first[:, 0]], 1)
    starts = turn_of(np.arange(0, length, chunk, dtype=np.int64), channels, length)
    steps = np.concatenate([np.stack([starts[:, part]] * PARTS, 1) for part in range(PARTS)], -1)
    steps = steps.reshape(-1, steps.shape[-1])
    steps = np.pad(steps, ((0, 0), (0, -steps.shape[1] % LANES)))
    return np.concatenate([x.reshape(steps.shape[0], -1) for x in (first, crossed, steps)], 1).astype(np.float32)


def transform_kernel(chunk, voltages_hbm, taps_hbm, twiddle_hbm, out_ref, volts, taps_ref, table, weights, sems):
    length = volts.shape[0]
    chunks = length // chunk
    taps = taps_ref.shape[0]
    rows = table.shape[0]
    per_block = PARTS * CH_DEV
    blocks = rows // per_block
    table_copy = pltpu.make_async_copy(twiddle_hbm, table, sems.at[0])
    taps_copy = pltpu.make_async_copy(taps_hbm, taps_ref, sems.at[1])
    table_copy.start()
    taps_copy.start()
    volts_copies = [
        pltpu.make_async_copy(
            voltages_hbm.at[pl.ds(step * chunk, chunk)], volts.at[pl.ds(step * chunk, chunk)], sems.at[2 + step]
        )
        for step in range(chunks)
    ]
    for copy in volts_copies:
        copy.start()
    table_copy.wait()
    taps_copy.wait()
    first, crossed = table[:, :chunk], table[:, chunk:2 * chunk]
    for step in range(chunks):
        part = pl.ds(step * chunk, chunk)
        turns = first
        if step:
            turns = first * table[:, 2 * chunk + step:2 * chunk + step + 1]
            step_sin = 2 * chunk + chunks + step
            turns = turns + crossed * table[:, step_sin:step_sin + 1]
        for t in range(taps):
            exact = turns * taps_ref[t:t + 1, part]
            high = exact.astype(jnp.bfloat16)
            weights[t * rows:(t + 1) * rows, part] = high
            weights[(taps + t) * rows:(taps + t + 1) * rows, part] = (
                exact - high.astype(jnp.float32)
            ).astype(jnp.bfloat16)
    total = jnp.zeros((2 * taps * rows, volts.shape[1]), jnp.float32)
    start = 0
    for eighths in ENDS:
        stop = chunks * eighths // 8
        if stop == start:
            continue
        for copy in volts_copies[start:stop]:
            copy.wait()
        part = pl.ds(start * chunk, (stop - start) * chunk)
        total = total + jnp.dot(weights[:, part], volts[part], preferred_element_type=jnp.float32)
        start = stop
    total = total[:taps * rows] + total[taps * rows:]
    mine = lax.axis_index("chan")
    for block in range(blocks):
        pieces = [
            total[t * rows + block * per_block:t * rows + (block + 1) * per_block] for t in range(taps)
        ]
        out_ref[lax.bitwise_xor(mine, block)] = jnp.concatenate(pieces, 0).astype(out_ref.dtype)


def transform(voltages, filter_taps):
    length, inputs = voltages.shape
    taps = filter_taps.shape[0]
    chunk = min(length, CHUNK)
    chunks = length // chunk
    blocks = lax.axis_size("chan")
    twiddle = jnp.asarray(twiddle_tables(length, blocks, chunk))
    per_block = PARTS * CH_DEV
    rows = blocks * per_block
    return pl.pallas_call(
        functools.partial(transform_kernel, chunk),
        out_shape=jax.ShapeDtypeStruct((blocks, taps * per_block, inputs), jnp.bfloat16),
        in_specs=[pl.BlockSpec(memory_space=pltpu.HBM)] * 3,
        out_specs=pl.BlockSpec(memory_space=pltpu.VMEM),
        scratch_shapes=[
            pltpu.VMEM((length, inputs), jnp.bfloat16),
            pltpu.VMEM((taps, length), jnp.float32),
            pltpu.VMEM(twiddle.shape, jnp.float32),
            pltpu.VMEM((2 * taps * rows, length), jnp.bfloat16),
            pltpu.SemaphoreType.DMA((2 + chunks,)),
        ],
        compiler_params=pltpu.CompilerParams(vmem_limit_bytes=int(53.8 * 2**20)),
        name="transform",
    )(voltages, filter_taps, twiddle)


def moved(array, frame_bits, swap):
    chans, groups = lax.axis_size("chan"), lax.axis_size("tgrp")
    count = chans * groups * 2
    return lax.ppermute(array, AXES, [(i, i ^ (frame_bits * 2 + swap)) for i in range(count)])


def exchanged(terms):
    chans, groups = lax.axis_size("chan"), lax.axis_size("tgrp")
    held = {0: (terms, 0)}
    bits = [groups << b for b in reversed(range(chans.bit_length() - 1))]
    bits += [1 << b for b in reversed(range(groups.bit_length() - 1))]
    rounds = [bits[:len(bits) % 2]] + [bits[i:i + 2] for i in range(len(bits) % 2, len(bits), 2)]
    for bits in rounds:
        of_chan = [bit for bit in bits if bit >= groups]

        def blocks_for(value, mask):
            count = value.shape[0] >> len(of_chan)
            index = sum(1 << i for i, bit in enumerate(reversed(of_chan)) if mask & bit)
            return value[index * count:(index + 1) * count]

        kept = {frame: (blocks_for(value, 0), half) for frame, (value, half) in held.items()}
        masks = [sum(bit for i, bit in enumerate(bits) if pick >> i & 1) for pick in range(1, 1 << len(bits))]
        for mask in reversed(masks):
            got = moved(jnp.concatenate([blocks_for(value, mask) for value, _ in held.values()], 0), mask, 1)
            count = got.shape[0] // len(held)
            for index, (frame, (_, half)) in enumerate(held.items()):
                kept[frame ^ mask] = (got[index * count:(index + 1) * count], 1 - half)
        held = kept
    order = sorted(held)
    return jnp.concatenate([held[frame][0] for frame in order], 0), [held[frame][1] for frame in order]


def power_kernel(taps, groups, scale, halves, had_ref, got_ref, out_hbm, terms, made, sems):
    frames, columns = terms.shape[1], terms.shape[3]
    per_tap = PARTS * CH_DEV
    tiles = columns // LANES
    for frame, half in enumerate(halves):
        terms[half, frame] = had_ref[frame]
        terms[1 - half, frame] = got_ref[frame]
    group = lax.axis_index("tgrp")
    mine = lax.axis_index("chan") * groups + group
    rows = 2 * columns // groups
    left_start = group * rows
    left_half = lax.bitwise_xor(left_start // columns, lax.axis_index("pol"))

    def spectra_of(half):
        loaded = [terms[half, lax.bitwise_xor(mine, frame)].astype(jnp.float32) for frame in range(frames)]
        spectra = []
        for frame in range(frames):
            total = None
            for tap in range(taps):
                source = frame - (taps - 1) + tap
                if source >= 0:
                    term = loaded[source][tap * per_tap:(tap + 1) * per_tap]
                    total = term if total is None else total + term
            spectra.append(total)
        return spectra

    left = jnp.concatenate(spectra_of(left_half), 0)
    if rows != columns:
        left = pltpu.roll(left, columns - left_start % columns, 1)[:, :rows]
    right = spectra_of(0)
    turned = jnp.concatenate([x for s in right for x in (-s[CH_DEV:], s[:CH_DEV])], 0)
    right = jnp.concatenate(right, 0)
    channel_of = lax.broadcasted_iota(jnp.int32, right.shape, 0) % CH_DEV
    against = jnp.concatenate(
        [
            jnp.where(channel_of == channel, x, 0.0)[:, tile * LANES:(tile + 1) * LANES]
            for channel in range(CH_DEV)
            for tile in range(tiles)
            for x in (right, turned)
        ],
        1,
    ).astype(jnp.bfloat16)
    left = left.astype(jnp.bfloat16)
    per_row = CH_DEV * tiles * PARTS
    part_rows = max(rows // WRITES, 8)
    copies = []
    for step in range(rows // part_rows):
        product = scale * lax.dot_general(
            left[:, step * part_rows:(step + 1) * part_rows],
            against,
            (((0,), (0,)), ((), ())),
            preferred_element_type=jnp.float32,
        )
        start = step * part_rows * per_row
        for index in range(per_row):
            made[pl.ds(start + index, part_rows, stride=per_row), :] = product[:, index * LANES:(index + 1) * LANES]
        span = pl.ds(start, part_rows * per_row)
        copies.append(pltpu.make_async_copy(made.at[span], out_hbm.at[span], sems.at[step]))
        copies[-1].start()
    for copy in copies:
        copy.wait()


def powers(had, halves, taps):
    groups = lax.axis_size("tgrp")
    frames, depth, columns = had.shape
    rows = 2 * columns // groups
    tiles = columns // LANES
    out = pl.pallas_call(
        functools.partial(power_kernel, taps, groups, 1.0 / frames, halves),
        out_shape=jax.ShapeDtypeStruct((rows * CH_DEV * tiles * PARTS, LANES), jnp.float32),
        in_specs=[pl.BlockSpec(memory_space=pltpu.VMEM)] * 2,
        out_specs=pl.BlockSpec(memory_space=pltpu.HBM),
        scratch_shapes=[
            pltpu.VMEM((2, frames, depth, columns), jnp.bfloat16),
            pltpu.VMEM(((rows + 1) * CH_DEV * tiles * PARTS, LANES), jnp.float32),
            pltpu.SemaphoreType.DMA((WRITES,)),
        ],
        compiler_params=pltpu.CompilerParams(vmem_limit_bytes=32 * 2**20),
        name="powers",
    )(had, moved(had, 0, 1))
    out = out.reshape(rows, CH_DEV, tiles, PARTS, LANES).transpose(0, 1, 3, 2, 4)
    return out.reshape(rows, CH_DEV, PARTS, columns)


def body(voltages, filter_taps):
    terms = transform(voltages[0], filter_taps)
    had, halves = exchanged(terms)
    return powers(had, halves, filter_taps.shape[0])


def solution(mesh):
    return jax.shard_map(
        body,
        mesh=mesh,
        in_specs=(P(("beam", "chan", "tgrp"), None, "pol"), P()),
        out_specs=P("tgrp", ("beam", "chan"), None, "pol"),
        check_vma=False,
    )
```

```python
import functools
import math

import jax
import jax.numpy as jnp
import numpy as np
from jax import lax
from jax.experimental import pallas as pl
from jax.experimental.pallas import tpu as pltpu
from jax.sharding import PartitionSpec as P

BAND_START = 1024
CH_DEV = 2
PARTS = 2
LANES = 128
CHUNK = 1024
ENDS = (1, 3, 6, 8)
WRITES = 4
AXES = ("chan", "tgrp", "pol")


def turn_of(samples, channels, length):
    phase = (channels[:, None] * samples) % length
    angles = phase * (2.0 * math.pi / length)
    both = np.stack([np.cos(angles), -np.sin(angles)], 0)
    return both.reshape(PARTS, -1, CH_DEV, samples.size).transpose(1, 0, 2, 3)


def twiddle_tables(length, blocks, chunk):
    channels = BAND_START + np.arange(blocks * CH_DEV, dtype=np.int64)
    first = turn_of(np.arange(chunk, dtype=np.int64), channels, length)
    crossed = np.stack([-first[:, 1], first[:, 0]], 1)
    starts = turn_of(np.arange(0, length, chunk, dtype=np.int64), channels, length)
    steps = np.concatenate([np.stack([starts[:, part]] * PARTS, 1) for part in range(PARTS)], -1)
    steps = steps.reshape(-1, steps.shape[-1])
    steps = np.pad(steps, ((0, 0), (0, -steps.shape[1] % LANES)))
    return np.concatenate([x.reshape(steps.shape[0], -1) for x in (first, crossed, steps)], 1).astype(np.float32)


def transform_kernel(chunk, voltages_hbm, taps_hbm, twiddle_hbm, out_ref, volts, taps_ref, table, weights, sems):
    length = volts.shape[0]
    chunks = length // chunk
    taps = taps_ref.shape[0]
    rows = table.shape[0]
    per_block = PARTS * CH_DEV
    blocks = rows // per_block
    table_copy = pltpu.make_async_copy(twiddle_hbm, table, sems.at[0])
    taps_copy = pltpu.make_async_copy(taps_hbm, taps_ref, sems.at[1])
    table_copy.start()
    taps_copy.start()
    volts_copies = [
        pltpu.make_async_copy(
            voltages_hbm.at[pl.ds(step * chunk, chunk)], volts.at[pl.ds(step * chunk, chunk)], sems.at[2 + step]
        )
        for step in range(chunks)
    ]
    for copy in volts_copies:
        copy.start()
    table_copy.wait()
    taps_copy.wait()
    first, crossed = table[:, :chunk], table[:, chunk:2 * chunk]
    for step in range(chunks):
        part = pl.ds(step * chunk, chunk)
        turns = first
        if step:
            turns = first * table[:, 2 * chunk + step:2 * chunk + step + 1]
            step_sin = 2 * chunk + chunks + step
            turns = turns + crossed * table[:, step_sin:step_sin + 1]
        for t in range(taps):
            exact = turns * taps_ref[t:t + 1, part]
            high = exact.astype(jnp.bfloat16)
            weights[t * rows:(t + 1) * rows, part] = high
            weights[(taps + t) * rows:(taps + t + 1) * rows, part] = (
                exact - high.astype(jnp.float32)
            ).astype(jnp.bfloat16)
    total = jnp.zeros((2 * taps * rows, volts.shape[1]), jnp.float32)
    start = 0
    for eighths in ENDS:
        stop = chunks * eighths // 8
        if stop == start:
            continue
        for copy in volts_copies[start:stop]:
            copy.wait()
        part = pl.ds(start * chunk, (stop - start) * chunk)
        total = total + jnp.dot(weights[:, part], volts[part], preferred_element_type=jnp.float32)
        start = stop
    total = total[:taps * rows] + total[taps * rows:]
    mine = lax.axis_index("chan")
    for block in range(blocks):
        pieces = [
            total[t * rows + block * per_block:t * rows + (block + 1) * per_block] for t in range(taps)
        ]
        out_ref[lax.bitwise_xor(mine, block)] = jnp.concatenate(pieces, 0).astype(out_ref.dtype)


def transform(voltages, filter_taps):
    length, inputs = voltages.shape
    taps = filter_taps.shape[0]
    chunk = min(length, CHUNK)
    chunks = length // chunk
    blocks = lax.axis_size("chan")
    twiddle = jnp.asarray(twiddle_tables(length, blocks, chunk))
    per_block = PARTS * CH_DEV
    rows = blocks * per_block
    return pl.pallas_call(
        functools.partial(transform_kernel, chunk),
        out_shape=jax.ShapeDtypeStruct((blocks, taps * per_block, inputs), jnp.bfloat16),
        in_specs=[pl.BlockSpec(memory_space=pltpu.HBM)] * 3,
        out_specs=pl.BlockSpec(memory_space=pltpu.VMEM),
        scratch_shapes=[
            pltpu.VMEM((length, inputs), jnp.bfloat16),
            pltpu.VMEM((taps, length), jnp.float32),
            pltpu.VMEM(twiddle.shape, jnp.float32),
            pltpu.VMEM((2 * taps * rows, length), jnp.bfloat16),
            pltpu.SemaphoreType.DMA((2 + chunks,)),
        ],
        compiler_params=pltpu.CompilerParams(vmem_limit_bytes=int(53.8 * 2**20)),
        name="transform",
    )(voltages, filter_taps, twiddle)


def moved(array, masks):
    devices = lax.axis_size("chan") * lax.axis_size("tgrp") * 2
    return lax.ppermute(array, AXES, [(i, i ^ (masks[i % 2] * 2 + 1)) for i in range(devices)])


def swapped(payloads, one, other):
    first = lax.axis_index("pol") == 0
    early = moved(jnp.where(first, payloads[one], payloads[other]), (one, other))
    late = moved(jnp.where(first, payloads[other], payloads[one]), (other, one))
    return {one: jnp.where(first, late, early), other: jnp.where(first, early, late)}


def exchanged(terms):
    chans, groups = lax.axis_size("chan"), lax.axis_size("tgrp")
    held = {0: (terms, 0)}
    bits = [groups << b for b in reversed(range(chans.bit_length() - 1))]
    bits += [1 << b for b in reversed(range(groups.bit_length() - 1))]
    rounds = [bits[:len(bits) % 2]] + [bits[i:i + 2] for i in range(len(bits) % 2, len(bits), 2)]
    for bits in rounds:
        of_chan = [bit for bit in bits if bit >= groups]

        def blocks_for(value, mask):
            count = value.shape[0] >> len(of_chan)
            index = sum(1 << i for i, bit in enumerate(reversed(of_chan)) if mask & bit)
            return value[index * count:(index + 1) * count]

        def payload(mask):
            return jnp.concatenate([blocks_for(value, mask) for value, _ in held.values()], 0)

        got = {}
        if len(bits) == 2:
            high, low = bits
            got = swapped({mask: payload(mask) for mask in bits}, low, high)
        if bits:
            got[sum(bits)] = moved(payload(sum(bits)), (sum(bits),) * 2)
        kept = {frame: (blocks_for(value, 0), half) for frame, (value, half) in held.items()}
        for mask, value in got.items():
            count = value.shape[0] // len(held)
            for index, (frame, (_, half)) in enumerate(held.items()):
                kept[frame ^ mask] = (value[index * count:(index + 1) * count], 1 - half)
        held = kept
    order = sorted(held)
    return jnp.concatenate([held[frame][0] for frame in order], 0), [held[frame][1] for frame in order]


def power_kernel(taps, groups, scale, halves, had_ref, got_ref, out_hbm, terms, made, sems):
    frames, columns = terms.shape[1], terms.shape[3]
    per_tap = PARTS * CH_DEV
    tiles = columns // LANES
    for frame, half in enumerate(halves):
        terms[half, frame] = had_ref[frame]
        terms[1 - half, frame] = got_ref[frame]
    group = lax.axis_index("tgrp")
    mine = lax.axis_index("chan") * groups + group
    rows = 2 * columns // groups
    left_start = group * rows
    left_half = lax.bitwise_xor(left_start // columns, lax.axis_index("pol"))

    def spectra_of(half):
        loaded = [terms[half, lax.bitwise_xor(mine, frame)].astype(jnp.float32) for frame in range(frames)]
        spectra = []
        for frame in range(frames):
            total = None
            for tap in range(taps):
                source = frame - (taps - 1) + tap
                if source >= 0:
                    term = loaded[source][tap * per_tap:(tap + 1) * per_tap]
                    total = term if total is None else total + term
            spectra.append(total)
        return spectra

    left = jnp.concatenate(spectra_of(left_half), 0)
    if rows != columns:
        left = pltpu.roll(left, columns - left_start % columns, 1)[:, :rows]
    right = spectra_of(0)
    turned = jnp.concatenate([x for s in right for x in (-s[CH_DEV:], s[:CH_DEV])], 0)
    right = jnp.concatenate(right, 0)
    channel_of = lax.broadcasted_iota(jnp.int32, right.shape, 0) % CH_DEV
    against = jnp.concatenate(
        [
            jnp.where(channel_of == channel, x, 0.0)[:, tile * LANES:(tile + 1) * LANES]
            for channel in range(CH_DEV)
            for tile in range(tiles)
            for x in (right, turned)
        ],
        1,
    ).astype(jnp.bfloat16)
    left = left.astype(jnp.bfloat16)
    per_row = CH_DEV * tiles * PARTS
    part_rows = max(rows // WRITES, 8)
    copies = []
    for step in range(rows // part_rows):
        product = scale * lax.dot_general(
            left[:, step * part_rows:(step + 1) * part_rows],
            against,
            (((0,), (0,)), ((), ())),
            preferred_element_type=jnp.float32,
        )
        start = step * part_rows * per_row
        for index in range(per_row):
            made[pl.ds(start + index, part_rows, stride=per_row), :] = product[:, index * LANES:(index + 1) * LANES]
        span = pl.ds(start, part_rows * per_row)
        copies.append(pltpu.make_async_copy(made.at[span], out_hbm.at[span], sems.at[step]))
        copies[-1].start()
    for copy in copies:
        copy.wait()


def powers(had, halves, taps):
    groups = lax.axis_size("tgrp")
    frames, depth, columns = had.shape
    rows = 2 * columns // groups
    tiles = columns // LANES
    out = pl.pallas_call(
        functools.partial(power_kernel, taps, groups, 1.0 / frames, halves),
        out_shape=jax.ShapeDtypeStruct((rows * CH_DEV * tiles * PARTS, LANES), jnp.float32),
        in_specs=[pl.BlockSpec(memory_space=pltpu.VMEM)] * 2,
        out_specs=pl.BlockSpec(memory_space=pltpu.HBM),
        scratch_shapes=[
            pltpu.VMEM((2, frames, depth, columns), jnp.bfloat16),
            pltpu.VMEM(((rows + 1) * CH_DEV * tiles * PARTS, LANES), jnp.float32),
            pltpu.SemaphoreType.DMA((WRITES,)),
        ],
        compiler_params=pltpu.CompilerParams(vmem_limit_bytes=32 * 2**20),
        name="powers",
    )(had, moved(had, (0, 0)))
    out = out.reshape(rows, CH_DEV, tiles, PARTS, LANES).transpose(0, 1, 3, 2, 4)
    return out.reshape(rows, CH_DEV, PARTS, columns)


def body(voltages, filter_taps):
    terms = transform(voltages[0], filter_taps)
    had, halves = exchanged(terms)
    return powers(had, halves, filter_taps.shape[0])


def solution(mesh):
    return jax.shard_map(
        body,
        mesh=mesh,
        in_specs=(P(("beam", "chan", "tgrp"), None, "pol"), P()),
        out_specs=P("tgrp", ("beam", "chan"), None, "pol"),
        check_vma=False,
    )
```

```python
import functools
import math

import jax
import jax.numpy as jnp
import numpy as np
from jax import lax
from jax.experimental import pallas as pl
from jax.experimental.pallas import tpu as pltpu
from jax.sharding import PartitionSpec as P

BAND_START = 1024
CH_DEV = 2
PARTS = 2
LANES = 128
CHUNK = 1024
ENDS = (1, 3, 6, 8)
WRITES = 4
AXES = ("chan", "tgrp", "pol")


def turn_of(samples, channels, length):
    phase = (channels[:, None] * samples) % length
    angles = phase * (2.0 * math.pi / length)
    both = np.stack([np.cos(angles), -np.sin(angles)], 0)
    return both.reshape(PARTS, -1, CH_DEV, samples.size).transpose(1, 0, 2, 3)


def twiddle_tables(length, blocks, chunk):
    channels = BAND_START + np.arange(blocks * CH_DEV, dtype=np.int64)
    first = turn_of(np.arange(chunk, dtype=np.int64), channels, length)
    crossed = np.stack([-first[:, 1], first[:, 0]], 1)
    starts = turn_of(np.arange(0, length, chunk, dtype=np.int64), channels, length)
    steps = np.concatenate([np.stack([starts[:, part]] * PARTS, 1) for part in range(PARTS)], -1)
    steps = steps.reshape(-1, steps.shape[-1])
    steps = np.pad(steps, ((0, 0), (0, -steps.shape[1] % LANES)))
    return np.concatenate([x.reshape(steps.shape[0], -1) for x in (first, crossed, steps)], 1).astype(np.float32)


def transform_kernel(chunk, voltages_hbm, taps_hbm, twiddle_hbm, out_ref, volts, taps_ref, table, weights, sems):
    length = volts.shape[0]
    chunks = length // chunk
    taps = taps_ref.shape[0]
    rows = table.shape[0]
    per_block = PARTS * CH_DEV
    blocks = rows // per_block
    table_copy = pltpu.make_async_copy(twiddle_hbm, table, sems.at[0])
    taps_copy = pltpu.make_async_copy(taps_hbm, taps_ref, sems.at[1])
    table_copy.start()
    taps_copy.start()
    volts_copies = [
        pltpu.make_async_copy(
            voltages_hbm.at[pl.ds(step * chunk, chunk)], volts.at[pl.ds(step * chunk, chunk)], sems.at[2 + step]
        )
        for step in range(chunks)
    ]
    for copy in volts_copies:
        copy.start()
    table_copy.wait()
    taps_copy.wait()
    first, crossed = table[:, :chunk], table[:, chunk:2 * chunk]
    for step in range(chunks):
        part = pl.ds(step * chunk, chunk)
        turns = first
        if step:
            turns = first * table[:, 2 * chunk + step:2 * chunk + step + 1]
            step_sin = 2 * chunk + chunks + step
            turns = turns + crossed * table[:, step_sin:step_sin + 1]
        for t in range(taps):
            exact = turns * taps_ref[t:t + 1, part]
            high = exact.astype(jnp.bfloat16)
            weights[t * rows:(t + 1) * rows, part] = high
            weights[(taps + t) * rows:(taps + t + 1) * rows, part] = (
                exact - high.astype(jnp.float32)
            ).astype(jnp.bfloat16)
    total = jnp.zeros((2 * taps * rows, volts.shape[1]), jnp.float32)
    start = 0
    for eighths in ENDS:
        stop = chunks * eighths // 8
        if stop == start:
            continue
        for copy in volts_copies[start:stop]:
            copy.wait()
        part = pl.ds(start * chunk, (stop - start) * chunk)
        total = total + jnp.dot(weights[:, part], volts[part], preferred_element_type=jnp.float32)
        start = stop
    total = total[:taps * rows] + total[taps * rows:]
    mine = lax.axis_index("chan")
    for block in range(blocks):
        pieces = [
            total[t * rows + block * per_block:t * rows + (block + 1) * per_block] for t in range(taps)
        ]
        out_ref[lax.bitwise_xor(mine, block)] = jnp.concatenate(pieces, 0).astype(out_ref.dtype)


def transform(voltages, filter_taps):
    length, inputs = voltages.shape
    taps = filter_taps.shape[0]
    chunk = min(length, CHUNK)
    chunks = length // chunk
    blocks = lax.axis_size("chan")
    twiddle = jnp.asarray(twiddle_tables(length, blocks, chunk))
    per_block = PARTS * CH_DEV
    rows = blocks * per_block
    return pl.pallas_call(
        functools.partial(transform_kernel, chunk),
        out_shape=jax.ShapeDtypeStruct((blocks, taps * per_block, inputs), jnp.bfloat16),
        in_specs=[pl.BlockSpec(memory_space=pltpu.HBM)] * 3,
        out_specs=pl.BlockSpec(memory_space=pltpu.VMEM),
        scratch_shapes=[
            pltpu.VMEM((length, inputs), jnp.bfloat16),
            pltpu.VMEM((taps, length), jnp.float32),
            pltpu.VMEM(twiddle.shape, jnp.float32),
            pltpu.VMEM((2 * taps * rows, length), jnp.bfloat16),
            pltpu.SemaphoreType.DMA((2 + chunks,)),
        ],
        compiler_params=pltpu.CompilerParams(vmem_limit_bytes=int(53.8 * 2**20)),
        name="transform",
    )(voltages, filter_taps, twiddle)


def moved(array, masks):
    devices = lax.axis_size("chan") * lax.axis_size("tgrp") * 2
    return lax.ppermute(array, AXES, [(i, i ^ (masks[i % 2] * 2 + 1)) for i in range(devices)])


def swapped(payloads, one, other):
    first = lax.axis_index("pol") == 0
    early = moved(jnp.where(first, payloads[one], payloads[other]), (one, other))
    late = moved(jnp.where(first, payloads[other], payloads[one]), (other, one))
    return {one: jnp.where(first, late, early), other: jnp.where(first, early, late)}


def exchanged(terms):
    chans, groups = lax.axis_size("chan"), lax.axis_size("tgrp")
    held = {0: (terms, 0)}
    bits = [groups << b for b in reversed(range(chans.bit_length() - 1))]
    bits += [1 << b for b in reversed(range(groups.bit_length() - 1))]
    rounds = [bits[:len(bits) % 2]] + [bits[i:i + 2] for i in range(len(bits) % 2, len(bits), 2)]
    for bits in rounds:
        of_chan = [bit for bit in bits if bit >= groups]

        def blocks_for(value, mask):
            count = value.shape[0] >> len(of_chan)
            index = sum(1 << i for i, bit in enumerate(reversed(of_chan)) if mask & bit)
            return value[index * count:(index + 1) * count]

        def payload(mask):
            return jnp.concatenate([blocks_for(value, mask) for value, _ in held.values()], 0)

        got = {}
        if len(bits) == 2:
            high, low = bits
            got = swapped({mask: payload(mask) for mask in bits}, low, high)
        if bits:
            got[sum(bits)] = moved(payload(sum(bits)), (sum(bits),) * 2)
        kept = {frame: (blocks_for(value, 0), half) for frame, (value, half) in held.items()}
        for mask, value in got.items():
            count = value.shape[0] // len(held)
            for index, (frame, (_, half)) in enumerate(held.items()):
                kept[frame ^ mask] = (value[index * count:(index + 1) * count], 1 - half)
        held = kept
    return jnp.concatenate([value for value, _ in held.values()], 0), [(frame, half) for frame, (_, half) in held.items()]


def power_kernel(taps, groups, scale, order, had_ref, got_ref, out_hbm, terms, made, sems):
    frames, columns = terms.shape[1], terms.shape[3]
    per_tap = PARTS * CH_DEV
    tiles = columns // LANES
    for position, (frame, half) in enumerate(order):
        terms[half, frame] = had_ref[position]
        terms[1 - half, frame] = got_ref[position]
    group = lax.axis_index("tgrp")
    mine = lax.axis_index("chan") * groups + group
    rows = 2 * columns // groups
    left_start = group * rows
    left_half = lax.bitwise_xor(left_start // columns, lax.axis_index("pol"))

    def spectra_of(half):
        loaded = [terms[half, lax.bitwise_xor(mine, frame)].astype(jnp.float32) for frame in range(frames)]
        spectra = []
        for frame in range(frames):
            total = None
            for tap in range(taps):
                source = frame - (taps - 1) + tap
                if source >= 0:
                    term = loaded[source][tap * per_tap:(tap + 1) * per_tap]
                    total = term if total is None else total + term
            spectra.append(total)
        return spectra

    left = jnp.concatenate(spectra_of(left_half), 0)
    if rows != columns:
        left = pltpu.roll(left, columns - left_start % columns, 1)[:, :rows]
    right = spectra_of(0)
    turned = jnp.concatenate([x for s in right for x in (-s[CH_DEV:], s[:CH_DEV])], 0)
    right = jnp.concatenate(right, 0)
    channel_of = lax.broadcasted_iota(jnp.int32, right.shape, 0) % CH_DEV
    against = jnp.concatenate(
        [
            jnp.where(channel_of == channel, x, 0.0)[:, tile * LANES:(tile + 1) * LANES]
            for channel in range(CH_DEV)
            for tile in range(tiles)
            for x in (right, turned)
        ],
        1,
    ).astype(jnp.bfloat16)
    left = left.astype(jnp.bfloat16)
    per_row = CH_DEV * tiles * PARTS
    part_rows = max(rows // WRITES, 8)
    copies = []
    for step in range(rows // part_rows):
        product = scale * lax.dot_general(
            left[:, step * part_rows:(step + 1) * part_rows],
            against,
            (((0,), (0,)), ((), ())),
            preferred_element_type=jnp.float32,
        )
        start = step * part_rows * per_row
        for index in range(per_row):
            made[pl.ds(start + index, part_rows, stride=per_row), :] = product[:, index * LANES:(index + 1) * LANES]
        span = pl.ds(start, part_rows * per_row)
        copies.append(pltpu.make_async_copy(made.at[span], out_hbm.at[span], sems.at[step]))
        copies[-1].start()
    for copy in copies:
        copy.wait()


def powers(had, order, taps):
    groups = lax.axis_size("tgrp")
    frames, depth, columns = had.shape
    rows = 2 * columns // groups
    tiles = columns // LANES
    out = pl.pallas_call(
        functools.partial(power_kernel, taps, groups, 1.0 / frames, order),
        out_shape=jax.ShapeDtypeStruct((rows * CH_DEV * tiles * PARTS, LANES), jnp.float32),
        in_specs=[pl.BlockSpec(memory_space=pltpu.VMEM)] * 2,
        out_specs=pl.BlockSpec(memory_space=pltpu.HBM),
        scratch_shapes=[
            pltpu.VMEM((2, frames, depth, columns), jnp.bfloat16),
            pltpu.VMEM(((rows + 1) * CH_DEV * tiles * PARTS, LANES), jnp.float32),
            pltpu.SemaphoreType.DMA((WRITES,)),
        ],
        compiler_params=pltpu.CompilerParams(vmem_limit_bytes=32 * 2**20),
        name="powers",
    )(had, moved(had, (0, 0)))
    out = out.reshape(rows, CH_DEV, tiles, PARTS, LANES).transpose(0, 1, 3, 2, 4)
    return out.reshape(rows, CH_DEV, PARTS, columns)


def body(voltages, filter_taps):
    terms = transform(voltages[0], filter_taps)
    had, order = exchanged(terms)
    return powers(had, order, filter_taps.shape[0])


def solution(mesh):
    return jax.shard_map(
        body,
        mesh=mesh,
        in_specs=(P(("beam", "chan", "tgrp"), None, "pol"), P()),
        out_specs=P("tgrp", ("beam", "chan"), None, "pol"),
        check_vma=False,
    )
```

```python
import functools
import math

import jax
import jax.numpy as jnp
import numpy as np
from jax import lax
from jax.experimental import pallas as pl
from jax.experimental.pallas import tpu as pltpu
from jax.sharding import PartitionSpec as P

BAND_START = 1024
CH_DEV = 2
PARTS = 2
LANES = 128
CHUNK = 1024
ENDS = (1, 3, 6, 8)
WRITES = 4
AXES = ("chan", "tgrp", "pol")


def turn_of(samples, channels, length):
    phase = (channels[:, None] * samples) % length
    angles = phase * (2.0 * math.pi / length)
    both = np.stack([np.cos(angles), -np.sin(angles)], 0)
    return both.reshape(PARTS, -1, CH_DEV, samples.size).transpose(1, 0, 2, 3)


def twiddle_tables(length, blocks, chunk):
    channels = BAND_START + np.arange(blocks * CH_DEV, dtype=np.int64)
    first = turn_of(np.arange(chunk, dtype=np.int64), channels, length)
    crossed = np.stack([-first[:, 1], first[:, 0]], 1)
    starts = turn_of(np.arange(0, length, chunk, dtype=np.int64), channels, length)
    steps = np.concatenate([np.stack([starts[:, part]] * PARTS, 1) for part in range(PARTS)], -1)
    steps = steps.reshape(-1, steps.shape[-1])
    steps = np.pad(steps, ((0, 0), (0, -steps.shape[1] % LANES)))
    return np.concatenate([x.reshape(steps.shape[0], -1) for x in (first, crossed, steps)], 1).astype(np.float32)


def transform_kernel(chunk, voltages_hbm, taps_hbm, twiddle_hbm, out_ref, volts, taps_ref, table, weights, sems):
    length = volts.shape[0]
    chunks = length // chunk
    taps = taps_ref.shape[0]
    rows = table.shape[0]
    per_block = PARTS * CH_DEV
    blocks = rows // per_block
    table_copy = pltpu.make_async_copy(twiddle_hbm, table, sems.at[0])
    taps_copy = pltpu.make_async_copy(taps_hbm, taps_ref, sems.at[1])
    table_copy.start()
    taps_copy.start()
    volts_copies = [
        pltpu.make_async_copy(
            voltages_hbm.at[pl.ds(step * chunk, chunk)], volts.at[pl.ds(step * chunk, chunk)], sems.at[2 + step]
        )
        for step in range(chunks)
    ]
    for copy in volts_copies:
        copy.start()
    table_copy.wait()
    taps_copy.wait()
    first, crossed = table[:, :chunk], table[:, chunk:2 * chunk]
    for step in range(chunks):
        part = pl.ds(step * chunk, chunk)
        turns = first
        if step:
            turns = first * table[:, 2 * chunk + step:2 * chunk + step + 1]
            step_sin = 2 * chunk + chunks + step
            turns = turns + crossed * table[:, step_sin:step_sin + 1]
        for t in range(taps):
            exact = turns * taps_ref[t:t + 1, part]
            high = exact.astype(jnp.bfloat16)
            weights[t * rows:(t + 1) * rows, part] = high
            weights[(taps + t) * rows:(taps + t + 1) * rows, part] = (
                exact - high.astype(jnp.float32)
            ).astype(jnp.bfloat16)
    total = jnp.zeros((2 * taps * rows, volts.shape[1]), jnp.float32)
    start = 0
    for eighths in ENDS:
        stop = chunks * eighths // 8
        if stop == start:
            continue
        for copy in volts_copies[start:stop]:
            copy.wait()
        part = pl.ds(start * chunk, (stop - start) * chunk)
        total = total + jnp.dot(weights[:, part], volts[part], preferred_element_type=jnp.float32)
        start = stop
    total = total[:taps * rows] + total[taps * rows:]
    mine = lax.axis_index("chan")
    for block in range(blocks):
        pieces = [
            total[t * rows + block * per_block:t * rows + (block + 1) * per_block] for t in range(taps)
        ]
        out_ref[lax.bitwise_xor(mine, block)] = jnp.concatenate(pieces, 0).astype(out_ref.dtype)


def transform(voltages, filter_taps):
    length, inputs = voltages.shape
    taps = filter_taps.shape[0]
    chunk = min(length, CHUNK)
    chunks = length // chunk
    blocks = lax.axis_size("chan")
    twiddle = jnp.asarray(twiddle_tables(length, blocks, chunk))
    per_block = PARTS * CH_DEV
    rows = blocks * per_block
    return pl.pallas_call(
        functools.partial(transform_kernel, chunk),
        out_shape=jax.ShapeDtypeStruct((blocks, taps * per_block, inputs), jnp.bfloat16),
        in_specs=[pl.BlockSpec(memory_space=pltpu.HBM)] * 3,
        out_specs=pl.BlockSpec(memory_space=pltpu.VMEM),
        scratch_shapes=[
            pltpu.VMEM((length, inputs), jnp.bfloat16),
            pltpu.VMEM((taps, length), jnp.float32),
            pltpu.VMEM(twiddle.shape, jnp.float32),
            pltpu.VMEM((2 * taps * rows, length), jnp.bfloat16),
            pltpu.SemaphoreType.DMA((2 + chunks,)),
        ],
        compiler_params=pltpu.CompilerParams(vmem_limit_bytes=int(53.8 * 2**20)),
        name="transform",
    )(voltages, filter_taps, twiddle)


def moved(array, masks):
    devices = lax.axis_size("chan") * lax.axis_size("tgrp") * 2
    return lax.ppermute(array, AXES, [(i, i ^ (masks[i % 2] * 2 + 1)) for i in range(devices)])


def swapped(payloads, one, other):
    first = lax.axis_index("pol") == 0
    early = moved(jnp.where(first, payloads[one], payloads[other]), (one, other))
    late = moved(jnp.where(first, payloads[other], payloads[one]), (other, one))
    return {one: jnp.where(first, late, early), other: jnp.where(first, early, late)}


def exchanged(terms):
    chans, groups = lax.axis_size("chan"), lax.axis_size("tgrp")
    held = {0: (terms, 0)}
    bits = [groups << b for b in reversed(range(chans.bit_length() - 1))]
    bits += [1 << b for b in reversed(range(groups.bit_length() - 1))]
    rounds = [bits[:len(bits) % 2]] + [bits[i:i + 2] for i in range(len(bits) % 2, len(bits), 2)]
    for bits in rounds:
        of_chan = [bit for bit in bits if bit >= groups]

        def blocks_for(value, mask):
            count = value.shape[0] >> len(of_chan)
            index = sum(1 << i for i, bit in enumerate(reversed(of_chan)) if mask & bit)
            return value[index * count:(index + 1) * count]

        def payload(mask):
            return jnp.concatenate([blocks_for(value, mask) for value, _ in held.values()], 0)

        got = {}
        if len(bits) == 2:
            high, low = bits
            got = swapped({mask: payload(mask) for mask in bits}, low, high)
        if bits:
            got[sum(bits)] = moved(payload(sum(bits)), (sum(bits),) * 2)
        kept = {frame: (blocks_for(value, 0), half) for frame, (value, half) in held.items()}
        for mask, value in got.items():
            count = value.shape[0] // len(held)
            for index, (frame, (_, half)) in enumerate(held.items()):
                kept[frame ^ mask] = (value[index * count:(index + 1) * count], 1 - half)
        held = kept
    return jnp.concatenate([value for value, _ in held.values()], 0), [(frame, half) for frame, (_, half) in held.items()]


def power_kernel(taps, groups, scale, order, had_ref, got_ref, out_hbm, terms, made, sems):
    frames, columns = terms.shape[1], terms.shape[3]
    per_tap = PARTS * CH_DEV
    tiles = columns // LANES
    for position, (frame, half) in enumerate(order):
        terms[half, frame] = had_ref[position]
        terms[1 - half, frame] = got_ref[position]
    group = lax.axis_index("tgrp")
    mine = lax.axis_index("chan") * groups + group
    rows = 2 * columns // groups
    left_start = group * rows
    left_half = lax.bitwise_xor(left_start // columns, lax.axis_index("pol"))

    def spectra_of(half):
        loaded = [terms[half, lax.bitwise_xor(mine, frame)].astype(jnp.float32) for frame in range(frames)]
        spectra = []
        for frame in range(frames):
            total = None
            for tap in range(taps):
                source = frame - (taps - 1) + tap
                if source >= 0:
                    term = loaded[source][tap * per_tap:(tap + 1) * per_tap]
                    total = term if total is None else total + term
            spectra.append(total)
        return spectra

    left = jnp.concatenate(spectra_of(left_half), 0)
    if rows != columns:
        left = pltpu.roll(left, columns - left_start % columns, 1)[:, :rows]
    right = spectra_of(0)
    turned = jnp.concatenate([x for s in right for x in (-s[CH_DEV:], s[:CH_DEV])], 0)
    right = jnp.concatenate(right, 0)
    channel_of = lax.broadcasted_iota(jnp.int32, right.shape, 0) % CH_DEV
    against = jnp.concatenate(
        [
            jnp.where(channel_of == channel, x, 0.0)[:, tile * LANES:(tile + 1) * LANES]
            for channel in range(CH_DEV)
            for tile in range(tiles)
            for x in (right, turned)
        ],
        1,
    ).astype(jnp.bfloat16)
    left = left.astype(jnp.bfloat16)
    per_row = CH_DEV * tiles * PARTS
    shares = [rows // 8, rows // 4, rows // 4, rows - rows // 8 - rows // 2]
    at = 0
    copies = []
    for step, part_rows in enumerate(shares):
        product = scale * lax.dot_general(
            left[:, at:at + part_rows],
            against,
            (((0,), (0,)), ((), ())),
            preferred_element_type=jnp.float32,
        )
        start = at * per_row
        at += part_rows
        for index in range(per_row):
            made[pl.ds(start + index, part_rows, stride=per_row), :] = product[:, index * LANES:(index + 1) * LANES]
        span = pl.ds(start, part_rows * per_row)
        copies.append(pltpu.make_async_copy(made.at[span], out_hbm.at[span], sems.at[step]))
        copies[-1].start()
    for copy in copies:
        copy.wait()


def powers(had, order, taps):
    groups = lax.axis_size("tgrp")
    frames, depth, columns = had.shape
    rows = 2 * columns // groups
    tiles = columns // LANES
    out = pl.pallas_call(
        functools.partial(power_kernel, taps, groups, 1.0 / frames, order),
        out_shape=jax.ShapeDtypeStruct((rows * CH_DEV * tiles * PARTS, LANES), jnp.float32),
        in_specs=[pl.BlockSpec(memory_space=pltpu.VMEM)] * 2,
        out_specs=pl.BlockSpec(memory_space=pltpu.HBM),
        scratch_shapes=[
            pltpu.VMEM((2, frames, depth, columns), jnp.bfloat16),
            pltpu.VMEM(((rows + 1) * CH_DEV * tiles * PARTS, LANES), jnp.float32),
            pltpu.SemaphoreType.DMA((WRITES,)),
        ],
        compiler_params=pltpu.CompilerParams(vmem_limit_bytes=32 * 2**20),
        name="powers",
    )(had, moved(had, (0, 0)))
    out = out.reshape(rows, CH_DEV, tiles, PARTS, LANES).transpose(0, 1, 3, 2, 4)
    return out.reshape(rows, CH_DEV, PARTS, columns)


def body(voltages, filter_taps):
    terms = transform(voltages[0], filter_taps)
    had, order = exchanged(terms)
    return powers(had, order, filter_taps.shape[0])


def solution(mesh):
    return jax.shard_map(
        body,
        mesh=mesh,
        in_specs=(P(("beam", "chan", "tgrp"), None, "pol"), P()),
        out_specs=P("tgrp", ("beam", "chan"), None, "pol"),
        check_vma=False,
    )
```
